32 devices in a mesh: leaf: 8 (over z, x), front: 4 (over y, core).
Axes of the slice: x: 2, y: 2, z: 4, core: 2. Of those that a mesh axis runs over, the one named last changes fastest.
Arguments:
- rhs_zero: float32 [64, 4096], P(None, 'leaf'), may hold values from -6 to 6
- rhs_one: float32 [64, 8192], P(None, 'leaf'), may hold values from -6 to 6
- rhs_two: float32 [64, 16384], P(None, 'leaf'), may hold values from -6 to 6
- pivot_zero: bfloat16 [4096, 4096], P('leaf', 'front'), may hold values from -0.09375 to 0.09375
- pivot_one: bfloat16 [8192, 4096], P('leaf', 'front'), may hold values from -0.09375 to 0.09375
- pivot_two: bfloat16 [16384, 4096], P('leaf', 'front'), may hold values from -0.09375 to 0.09375
- lower_one: bfloat16 [4096, 8192], P('front', 'leaf'), may hold values from -0.09375 to 0.09375
- lower_two: bfloat16 [4096, 16384], P('front', 'leaf'), may hold values from -0.09375 to 0.09375
- upper_one: bfloat16 [8192, 4096], P('leaf', 'front'), may hold values from -0.09375 to 0.09375
- upper_two: bfloat16 [16384, 4096], P('leaf', 'front'), may hold values from -0.09375 to 0.09375
- back_zero: bfloat16 [4096, 4096], P('front', 'leaf'), may hold values from -0.09375 to 0.09375
- back_one: bfloat16 [4096, 8192], P('front', 'leaf'), may hold values from -0.09375 to 0.09375
- back_two: bfloat16 [4096, 16384], P('front', 'leaf'), may hold values from -0.09375 to 0.09375
- index_one: int32 [2, 4096], replicated, may hold values from 0 to 4095, as said below
- index_two: int32 [4, 4096], replicated, may hold values from 0 to 8191, as said below
Outputs:
- solution_zero: float32 [64, 4096], P(None, 'leaf')
- solution_one: float32 [64, 8192], P(None, 'leaf')
- solution_two: float32 [64, 16384], P(None, 'leaf')
The draws below stay inside these ranges and needn't reach their ends.
Inputs may be any that keep to these rules, and one draw needn't show every extreme that they name: `index_one`: each row holds 4096 different columns of the root separator. `index_two`: each row holds 4096 different ancestor rows, coded as in the reference program.
All inputs are finite; a program needn't handle non-finite values.
Results may differ from the reference program's by a relative error of at most 0.013.
Values may be sent and summed in bfloat16 or wider, within the bound.
No kernel may reach another device: no remote copies, remote signals or barrier semaphores. Data moves between devices by JAX's collectives and lax.ppermute only.
A program may use at most 128 MiB of HBM per device.

```python
import jax
import jax.numpy as jnp
from jax import lax

SEP = 4096
UPD = 4096
RHS = 64


def pick_rows(key, fronts, extent):
    picked = []
    for front_id in range(fronts):
        front_key = jax.random.fold_in(key, front_id)
        middle = jax.random.permutation(jax.random.fold_in(front_key, 1), extent - 2)[:UPD - 2].astype(jnp.int32) + 1
        extremes = jnp.array([0, extent - 1], jnp.int32)
        joined = jnp.concatenate([extremes, middle])
        shuffle = jax.random.permutation(jax.random.fold_in(front_key, 2), UPD)
        picked.append(joined[shuffle])
    return jnp.stack(picked)


def draw_index_one(key, part):
    return pick_rows(jax.random.fold_in(key, 11), 2, SEP)


def draw_index_two(key, part):
    return pick_rows(jax.random.fold_in(key, 23), 4, 2 * SEP)


def shard_levels(key, shape, split, low, largest):
    gain = 1.0
    for axis_at, shards_of in split:
        steps = jax.random.uniform(jax.random.fold_in(jax.random.fold_in(key, 6), axis_at), (shards_of,), jnp.float32, low / len(split), largest / len(split))
        gain = gain * jnp.repeat(jnp.exp(steps), shape[axis_at] // shards_of).reshape((-1,) + (1,) * (len(shape) - 1 - axis_at))
    return gain


def gaussian(key, shape, deviation, bound, split=(), held_as=jnp.bfloat16):
    values = deviation * jax.random.normal(key, shape, jnp.float32)
    if split:
        values = values * shard_levels(key, shape, split, -0.22, 0.18)
    return jnp.clip(values, -bound, bound).astype(held_as)


def setup_inputs(seed: int = 0) -> dict:
    arg_keys = jax.random.split(jax.random.key(seed), 16)
    return {
        "rhs_zero": gaussian(arg_keys[0], (RHS, SEP), 1.0, 6.0, ((1, 8),), jnp.float32),
        "rhs_one": gaussian(arg_keys[1], (RHS, 2 * SEP), 1.0, 6.0, ((1, 8),), jnp.float32),
        "rhs_two": gaussian(arg_keys[2], (RHS, 4 * SEP), 1.0, 6.0, ((1, 8),), jnp.float32),
        "pivot_zero": gaussian(arg_keys[3], (SEP, SEP), SEP ** -0.5, 0.09375, ((0, 8), (1, 4))),
        "pivot_one": gaussian(arg_keys[4], (2 * SEP, SEP), SEP ** -0.5, 0.09375, ((0, 8), (1, 4))),
        "pivot_two": gaussian(arg_keys[5], (4 * SEP, SEP), SEP ** -0.5, 0.09375, ((0, 8), (1, 4))),
        "lower_one": gaussian(arg_keys[6], (SEP, 2 * UPD), SEP ** -0.5, 0.09375, ((0, 4), (1, 8))),
        "lower_two": gaussian(arg_keys[7], (SEP, 4 * UPD), SEP ** -0.5, 0.09375, ((0, 4), (1, 8))),
        "upper_one": gaussian(arg_keys[8], (2 * UPD, SEP), UPD ** -0.5, 0.09375, ((0, 8), (1, 4))),
        "upper_two": gaussian(arg_keys[9], (4 * UPD, SEP), UPD ** -0.5, 0.09375, ((0, 8), (1, 4))),
        "back_zero": gaussian(arg_keys[10], (SEP, SEP), SEP ** -0.5, 0.09375, ((0, 4), (1, 8))),
        "back_one": gaussian(arg_keys[11], (SEP, 2 * SEP), SEP ** -0.5, 0.09375, ((0, 4), (1, 8))),
        "back_two": gaussian(arg_keys[12], (SEP, 4 * SEP), SEP ** -0.5, 0.09375, ((0, 4), (1, 8))),
        "index_one": draw_index_one(jax.random.fold_in(arg_keys[15], 71), 0),
        "index_two": draw_index_two(jax.random.fold_in(arg_keys[15], 71), 0),
    }


def mat_product(left, right):
    return jnp.dot(left.astype(jnp.float32), right.astype(jnp.float32), precision=lax.Precision.HIGHEST, preferred_element_type=jnp.float32)


def front_columns(index_row, front_id, tier_index):
    level_of = index_row // SEP
    ancestor = jnp.right_shift(jnp.full_like(level_of, front_id), tier_index - level_of)
    base = jnp.left_shift(jnp.ones_like(level_of), level_of) - 1
    return (base + ancestor) * SEP + index_row % SEP


def reference(rhs_zero, rhs_one, rhs_two, pivot_zero, pivot_one, pivot_two, lower_one, lower_two, upper_one, upper_two, back_zero, back_one, back_two, index_one, index_two):
    rhs_list = (rhs_zero, rhs_one, rhs_two)
    pivot_list = (pivot_zero, pivot_one, pivot_two)
    lower_list = (None, lower_one, lower_two)
    upper_list = (None, upper_one, upper_two)
    back_list = (back_zero, back_one, back_two)
    index_list = (None, index_one, index_two)
    pending = jnp.zeros((RHS, 7 * SEP), jnp.float32)
    solved = {}
    for tier_index in (2, 1, 0):
        for front_id in range(2 ** tier_index):
            spot = (2 ** tier_index - 1 + front_id) * SEP
            local_rhs = rhs_list[tier_index][:, front_id * SEP:(front_id + 1) * SEP]
            reduced = (local_rhs - pending[:, spot:spot + SEP]).astype(jnp.bfloat16)
            result = mat_product(reduced, pivot_list[tier_index][front_id * SEP:(front_id + 1) * SEP])
            solved[(tier_index, front_id)] = result
            if tier_index > 0:
                update = mat_product(result.astype(jnp.bfloat16), lower_list[tier_index][:, front_id * UPD:(front_id + 1) * UPD])
                targets = front_columns(index_list[tier_index][front_id], front_id, tier_index)
                pending = pending.at[:, targets].add(update)
    known = jnp.zeros((RHS, 7 * SEP), jnp.bfloat16)
    outputs = []
    for tier_index in (0, 1, 2):
        pieces = []
        for front_id in range(2 ** tier_index):
            spot = (2 ** tier_index - 1 + front_id) * SEP
            remaining = solved[(tier_index, front_id)]
            if tier_index > 0:
                targets = front_columns(index_list[tier_index][front_id], front_id, tier_index)
                picked = known[:, targets]
                remaining = remaining - mat_product(picked, upper_list[tier_index][front_id * UPD:(front_id + 1) * UPD])
            answer = mat_product(remaining.astype(jnp.bfloat16), back_list[tier_index][:, front_id * SEP:(front_id + 1) * SEP])
            pieces.append(answer)
            known = known.at[:, spot:spot + SEP].set(answer.astype(jnp.bfloat16))
        outputs.append(jnp.concatenate(pieces, axis=1))
    return (outputs[0], outputs[1], outputs[2])
```

```python
import jax
import jax.numpy as jnp
from jax import lax
from jax.sharding import PartitionSpec as P

BF16 = jnp.bfloat16
F32 = jnp.float32


def dot(left, right):
    return jnp.dot(left, right, preferred_element_type=F32)


def bit_groups(bits):
    bits = list(bits)
    return [bits[i : i + 2] for i in range(0, len(bits), 2)]


def partner(x, axis, mask):
    return lax.ppermute(x, axis, [(i, i ^ mask) for i in range(lax.axis_size(axis))])


def exchange_sum(x, axis, groups):
    for group in groups:
        low = x.astype(BF16)
        parts = [low] + [partner(low, axis, m << group[0]) for m in range(1, 1 << len(group))]
        parts = [p.astype(F32) for p in parts]
        while len(parts) > 1:
            parts = [parts[i] + parts[i + 1] for i in range(0, len(parts), 2)]
        x = parts[0]
    return x


def scatter_sum(x, axis, groups):
    for group in groups:
        count = 1 << len(group)
        width = x.shape[1] // count
        total = x[:, :width]
        for m in range(1, count):
            piece = x[:, m * width : (m + 1) * width].astype(BF16)
            total = total + partner(piece, axis, m << group[0]).astype(F32)
        x = total
    return x


def gather_blocks(x, axis, groups):
    for group in reversed(groups):
        x = jnp.concatenate([x] + [partner(x, axis, m << group[0]) for m in range(1, 1 << len(group))], axis=1)
    return x


def relative_block(owner, me, groups):
    rel = owner ^ me
    place = jnp.zeros_like(rel)
    for group in groups:
        place = (place << len(group)) | (rel >> group[0] & ((1 << len(group)) - 1))
    return place


def one_hot_rows(place, width):
    hot = place[:, None] == lax.broadcasted_iota(jnp.int32, (place.shape[0], width), 1)
    return lax.optimization_barrier(hot.astype(BF16))


def one_hot_columns(place, height):
    hot = place[None, :] == lax.broadcasted_iota(jnp.int32, (height, place.shape[0]), 0)
    return lax.optimization_barrier(hot.astype(BF16))


def per_device(
    rhs_zero, rhs_one, rhs_two,
    pivot_zero, pivot_one, pivot_two,
    lower_one, lower_two,
    upper_one, upper_two,
    back_zero, back_one, back_two,
    index_one, index_two,
):
    sep = lower_one.shape[0] * lax.axis_size("front")
    leaves = lax.axis_size("leaf")
    me = lax.axis_index("leaf")
    front_pos = lax.axis_index("front")
    core = front_pos & 1
    leaf_bits = leaves.bit_length() - 1
    front_bits = lax.axis_size("front").bit_length() - 1
    groups = [bit_groups(range(leaf_bits - level)) for level in range(3)]
    away = bit_groups(range(1, front_bits))
    rhs = (rhs_zero, rhs_one, rhs_two)
    pivot = (pivot_zero, pivot_one, pivot_two)
    lower = (None, lower_one, lower_two)
    upper = (None, upper_one, upper_two)
    back = (back_zero, back_one, back_two)

    def own_index(level):
        table = index_one if level == 1 else index_two
        width = leaves >> level
        chunk = table.shape[1] // width
        start = (me & width - 1) * chunk
        return lax.dynamic_slice(table, (me >> (leaf_bits - level), start), (1, chunk))[0]

    def split_place(column, level):
        block = sep // (leaves >> level)
        half = block // 2
        owner = column // block
        mine = me & (leaves >> level) - 1
        rel = relative_block(owner, mine, groups[level])
        return ((column // half & 1) ^ core) * (sep // 2) + rel * half + column % half

    def whole_place(column, level):
        block = sep // (leaves >> level)
        mine = me & (leaves >> level) - 1
        rel = relative_block(column // block, mine, groups[level])
        return rel * block + column % block

    def both_halves(own):
        other = partner(own, "front", 1)
        return jnp.concatenate([jnp.where(core == 0, own, other), jnp.where(core == 0, other, own)], axis=1)

    def front_half(x):
        width = x.shape[1] // 2
        keep = jnp.where(core == 0, x[:, :width], x[:, width:])
        send = jnp.where(core == 0, x[:, width:], x[:, :width])
        return exchange_sum(keep + partner(send, "front", 1), "front", away)

    def front_sum(x):
        return exchange_sum(x + partner(x, "front", 1), "front", away)

    def row_total(pending, level):
        width = sep // 2
        total = pending[:, :width] + partner(pending[:, width:], "front", 1)
        return scatter_sum(total, "leaf", groups[level])

    def half_columns(x):
        width = x.shape[1] // 2
        return jnp.where(core == 0, x[:, :width], x[:, width:])

    def core_slice(index):
        half = index.shape[0] // 2
        return lax.dynamic_slice(index, (core * half,), (half,))

    index = core_slice(own_index(2))
    is_root = index < sep
    place_one = jnp.where(is_root, -1, split_place(index - sep, 1))
    place_root = jnp.where(is_root, split_place(index, 0), -1)
    y_two = exchange_sum(dot(rhs_two.astype(BF16), pivot_two), "leaf", groups[2])
    hot_one = one_hot_rows(place_one, sep)
    hot_root = one_hot_rows(place_root, sep)
    update = front_half(dot(y_two.astype(BF16), lower_two)).astype(BF16)
    pending_one = dot(update, hot_one)
    pending_root = dot(update, hot_root)

    own_rhs = half_columns(rhs_one)
    reduced = both_halves((own_rhs - row_total(pending_one, 1)).astype(BF16))
    y_one = exchange_sum(dot(reduced, pivot_one), "leaf", groups[1])
    hot_up = one_hot_rows(split_place(core_slice(own_index(1)), 0), sep)
    update = front_half(dot(y_one.astype(BF16), lower_one)).astype(BF16)
    pending_root = pending_root + dot(update, hot_up)

    own_rhs = half_columns(rhs_zero)
    reduced = both_halves((own_rhs - row_total(pending_root, 0)).astype(BF16))
    y_zero = exchange_sum(dot(reduced, pivot_zero), "leaf", groups[0])
    x_zero = front_sum(dot(y_zero.astype(BF16), back_zero))
    known_zero = gather_blocks(x_zero.astype(BF16), "leaf", groups[0])

    pick_one = one_hot_columns(whole_place(own_index(1), 0), sep)
    index = own_index(2)
    is_root = index < sep
    pick_root = one_hot_columns(jnp.where(is_root, whole_place(index, 0), -1), sep)
    pick_mid = one_hot_columns(jnp.where(is_root, -1, whole_place(index - sep, 1)), sep)
    picked = dot(known_zero, pick_one).astype(BF16)
    z_one = y_one - exchange_sum(dot(picked, upper_one), "leaf", groups[1])
    x_one = front_sum(dot(z_one.astype(BF16), back_one))
    known_one = gather_blocks(x_one.astype(BF16), "leaf", groups[1])

    picked = (dot(known_zero, pick_root) + dot(known_one, pick_mid)).astype(BF16)
    z_two = y_two - exchange_sum(dot(picked, upper_two), "leaf", groups[2])
    x_two = front_sum(dot(z_two.astype(BF16), back_two))
    return x_zero, x_one, x_two


def solution(mesh):
    by_leaf = P(None, "leaf")
    rows = P("leaf", "front")
    columns = P("front", "leaf")
    return jax.shard_map(
        per_device,
        mesh=mesh,
        in_specs=(by_leaf,) * 3 + (rows,) * 3 + (columns,) * 2 + (rows,) * 2 + (columns,) * 3 + (P(), P()),
        out_specs=(by_leaf,) * 3,
        check_vma=False,
    )
```

```python
import jax
import jax.numpy as jnp
from jax import lax
from jax.experimental import pallas as pl
from jax.experimental.pallas import tpu as pltpu
from jax.sharding import PartitionSpec as P

BF16 = jnp.bfloat16
F32 = jnp.float32


def dot(left, right):
    return jnp.dot(left, right, preferred_element_type=F32)


def bit_groups(bits):
    bits = list(bits)
    return [bits[i : i + 2] for i in range(0, len(bits), 2)]


def partner(x, axis, mask):
    return lax.ppermute(x, axis, [(i, i ^ mask) for i in range(lax.axis_size(axis))])


def exchange_sum(x, axis, groups):
    for group in groups:
        low = x.astype(BF16)
        parts = [low] + [partner(low, axis, m << group[0]) for m in range(1, 1 << len(group))]
        parts = [p.astype(F32) for p in parts]
        while len(parts) > 1:
            parts = [parts[i] + parts[i + 1] for i in range(0, len(parts), 2)]
        x = parts[0]
    return x


def scatter_sum(x, axis, groups):
    for group in groups:
        count = 1 << len(group)
        width = x.shape[1] // count
        total = x[:, :width]
        for m in range(1, count):
            piece = x[:, m * width : (m + 1) * width].astype(BF16)
            total = total + partner(piece, axis, m << group[0]).astype(F32)
        x = total
    return x


def gather_blocks(x, axis, groups):
    for group in groups[:0:-1]:
        x = jnp.concatenate([x] + [partner(x, axis, m << group[0]) for m in range(1, 1 << len(group))], axis=1)
    if not groups:
        return [x]
    return [x] + [partner(x, axis, m << groups[0][0]) for m in range(1, 1 << len(groups[0]))]


def relative_block(owner, me, groups):
    rel = owner ^ me
    place = jnp.zeros_like(rel)
    for group in groups:
        place = (place << len(group)) | (rel >> group[0] & ((1 << len(group)) - 1))
    return place


def one_hot_rows(place, width):
    hot = place[:, None] == lax.broadcasted_iota(jnp.int32, (place.shape[0], width), 1)
    return lax.optimization_barrier(hot.astype(BF16))


TILE = 256


def hot_tile(place, start, rows):
    rel = place - start
    rel = jnp.where((rel >= 0) & (rel < rows), rel, -1).astype(F32).astype(BF16)
    row = lax.broadcasted_iota(jnp.int32, (rows, place.shape[1]), 0).astype(F32).astype(BF16)
    return jnp.where(row == rel, jnp.ones((), BF16), jnp.zeros((), BF16))


def pick_kernel(*refs):
    pieces, (place_ref, block_ref, out_ref) = refs[:-3], refs[-3:]

    @pl.when(pl.program_id(0) == 0)
    def _():
        out_ref[...] = jnp.zeros_like(out_ref)

    place = place_ref[...]
    picked = jnp.zeros((out_ref.shape[0], place.shape[1]), F32)
    start = 0
    for piece in pieces:
        width = piece.shape[1]
        tile = min(TILE, width)
        for k in range(0, width, tile):
            picked += dot(piece[:, k : k + tile], hot_tile(place, start + k, tile))
        start += width
    out_ref[...] += dot(picked.astype(BF16), block_ref[...])


def picked_product(pieces, place, block):
    if pieces[0].shape[1] % TILE:
        pieces = [jnp.concatenate(pieces, axis=1)]
    rows, count, width = pieces[0].shape[0], place.shape[0], block.shape[1]
    step = min(count, 1024)
    extent = sum(p.shape[1] for p in pieces)
    return pl.pallas_call(
        pick_kernel,
        grid=(count // step,),
        in_specs=[pl.BlockSpec(p.shape, lambda i: (0, 0)) for p in pieces]
        + [pl.BlockSpec((1, step), lambda i: (0, i)), pl.BlockSpec((step, width), lambda i: (i, 0))],
        out_specs=pl.BlockSpec((rows, width), lambda i: (0, 0)),
        out_shape=jax.ShapeDtypeStruct((rows, width), F32),
        compiler_params=pltpu.CompilerParams(vmem_limit_bytes=16 << 20),
        cost_estimate=pl.CostEstimate(
            flops=2 * rows * count * (extent + width), bytes_accessed=2 * count * (width + 2 * extent), transcendentals=0
        ),
    )(*pieces, place[None, :], block)


def put_kernel(update_ref, place_ref, out_ref):
    update, place = update_ref[...], place_ref[...]
    step = out_ref.shape[1]
    base = pl.program_id(0) * step
    tile = min(TILE, step)
    for n in range(0, step, tile):
        hot = hot_tile(place, base + n, tile)
        out_ref[:, n : n + tile] = lax.dot_general(update, hot, (((1,), (1,)), ((), ())), preferred_element_type=F32)


def put_columns(update, place, width):
    rows, count = update.shape
    step = min(width, 2048)
    return pl.pallas_call(
        put_kernel,
        grid=(width // step,),
        in_specs=[pl.BlockSpec((rows, count), lambda i: (0, 0)), pl.BlockSpec((1, count), lambda i: (0, 0))],
        out_specs=pl.BlockSpec((rows, step), lambda i: (0, i)),
        out_shape=jax.ShapeDtypeStruct((rows, width), F32),
        compiler_params=pltpu.CompilerParams(vmem_limit_bytes=16 << 20),
        cost_estimate=pl.CostEstimate(flops=2 * rows * count * width, bytes_accessed=4 * count * width, transcendentals=0),
    )(update, place[None, :])


def per_device(
    rhs_zero, rhs_one, rhs_two,
    pivot_zero, pivot_one, pivot_two,
    lower_one, lower_two,
    upper_one, upper_two,
    back_zero, back_one, back_two,
    index_one, index_two,
):
    sep = lower_one.shape[0] * lax.axis_size("front")
    leaves = lax.axis_size("leaf")
    me = lax.axis_index("leaf")
    front_pos = lax.axis_index("front")
    core = front_pos & 1
    leaf_bits = leaves.bit_length() - 1
    front_bits = lax.axis_size("front").bit_length() - 1
    groups = [bit_groups(range(leaf_bits - level)) for level in range(3)]
    away = bit_groups(range(1, front_bits))

    def own_index(level):
        table = index_one if level == 1 else index_two
        width = leaves >> level
        chunk = table.shape[1] // width
        start = (me & width - 1) * chunk
        return lax.dynamic_slice(table, (me >> (leaf_bits - level), start), (1, chunk))[0]

    def split_place(column, level):
        block = sep // (leaves >> level)
        half = block // 2
        owner = column // block
        mine = me & (leaves >> level) - 1
        rel = relative_block(owner, mine, groups[level])
        return ((column // half & 1) ^ core) * (sep // 2) + rel * half + column % half

    def both_halves(own):
        other = partner(own, "front", 1)
        return in_order(own, other)

    def front_half(x):
        width = x.shape[1] // 2
        keep = jnp.where(core == 0, x[:, :width], x[:, width:])
        send = jnp.where(core == 0, x[:, width:], x[:, :width])
        return exchange_sum(keep + partner(send, "front", 1), "front", away)

    def in_order(own, other):
        return jnp.concatenate([jnp.where(core == 0, own, other), jnp.where(core == 0, other, own)], axis=1)

    def known_pieces(half, level):
        own = gather_blocks(half.astype(BF16), "leaf", groups[level])
        return own + [partner(piece, "front", 1) for piece in own]

    def row_total(pending, level):
        width = sep // 2
        total = pending[:, :width] + partner(pending[:, width:], "front", 1)
        return scatter_sum(total, "leaf", groups[level])

    def half_columns(x):
        width = x.shape[1] // 2
        return jnp.where(core == 0, x[:, :width], x[:, width:])

    def core_slice(index):
        half = index.shape[0] // 2
        return lax.dynamic_slice(index, (core * half,), (half,))

    index = own_index(2)
    is_root = index < sep
    place_one = jnp.where(is_root, -1, split_place(index - sep, 1))
    place_root = jnp.where(is_root, split_place(index, 0), -1)
    y_two = exchange_sum(dot(rhs_two.astype(BF16), pivot_two), "leaf", groups[2])
    hot_one = one_hot_rows(core_slice(place_one), sep)
    update = front_half(dot(y_two.astype(BF16), lower_two)).astype(BF16)
    pending_one = dot(update, hot_one)
    pending_root = put_columns(update, core_slice(place_root), sep)

    place_up = split_place(own_index(1), 0)
    own_rhs = half_columns(rhs_one)
    reduced = both_halves((own_rhs - row_total(pending_one, 1)).astype(BF16))
    y_one = exchange_sum(dot(reduced, pivot_one), "leaf", groups[1])
    hot_up = one_hot_rows(core_slice(place_up), sep)
    update = front_half(dot(y_one.astype(BF16), lower_one)).astype(BF16)
    pending_root = pending_root + dot(update, hot_up)

    near, far = groups[0][:1], groups[0][1:]
    count = 1 << len(near[0])
    block = pivot_zero.shape[1] // count
    starts = [((me & count - 1) ^ m) * block for m in range(count)]
    pivot_rel = jnp.concatenate([lax.dynamic_slice_in_dim(pivot_zero, at, block, 1) for at in starts], axis=1)
    back_rel = jnp.concatenate([lax.dynamic_slice_in_dim(back_zero, at, block, 0) for at in starts], axis=0)
    own_rhs = half_columns(rhs_zero)
    reduced = both_halves((own_rhs - row_total(pending_root, 0)).astype(BF16))
    y_zero = exchange_sum(scatter_sum(dot(reduced, pivot_rel), "leaf", near), "leaf", far)
    y_zero = jnp.concatenate(gather_blocks(y_zero.astype(BF16), "leaf", near), axis=1)
    x_zero = front_half(dot(y_zero, back_rel))
    known_zero = known_pieces(x_zero, 0)

    coupling = picked_product(known_zero, place_up, upper_one)
    z_one = y_one - exchange_sum(coupling, "leaf", groups[1])
    x_one = front_half(dot(z_one.astype(BF16), back_one))
    known_one = known_pieces(x_one, 1)

    coupling = picked_product(known_zero, place_root, upper_two) + picked_product(known_one, place_one, upper_two)
    z_two = y_two - exchange_sum(coupling, "leaf", groups[2])
    x_two = front_half(dot(z_two.astype(BF16), back_two))
    return both_halves(x_zero), both_halves(x_one), both_halves(x_two)


def solution(mesh):
    by_leaf = P(None, "leaf")
    rows = P("leaf", "front")
    columns = P("front", "leaf")
    return jax.shard_map(
        per_device,
        mesh=mesh,
        in_specs=(by_leaf,) * 3 + (rows,) * 3 + (columns,) * 2 + (rows,) * 2 + (columns,) * 3 + (P(), P()),
        out_specs=(by_leaf,) * 3,
        check_vma=False,
    )
```

```python
import functools

import jax
import jax.numpy as jnp
from jax import lax
from jax.experimental import pallas as pl
from jax.experimental.pallas import tpu as pltpu
from jax.sharding import PartitionSpec as P

BF16 = jnp.bfloat16
F32 = jnp.float32


def dot(left, right):
    return jnp.dot(left, right, preferred_element_type=F32)


def bit_groups(bits):
    bits = list(bits)
    return [bits[i : i + 2] for i in range(0, len(bits), 2)]


def partner(x, axis, mask):
    return lax.ppermute(x, axis, [(i, i ^ mask) for i in range(lax.axis_size(axis))])


def exchange_sum(x, axis, groups):
    for group in groups:
        low = x.astype(BF16)
        parts = [low] + [partner(low, axis, m << group[0]) for m in range(1, 1 << len(group))]
        parts = [p.astype(F32) for p in parts]
        while len(parts) > 1:
            parts = [parts[i] + parts[i + 1] for i in range(0, len(parts), 2)]
        x = parts[0]
    return x


def scatter_sum(x, axis, groups):
    for group in groups:
        count = 1 << len(group)
        width = x.shape[1] // count
        total = x[:, :width]
        for m in range(1, count):
            piece = x[:, m * width : (m + 1) * width].astype(BF16)
            total = total + partner(piece, axis, m << group[0]).astype(F32)
        x = total
    return x


def gather_blocks(x, axis, groups):
    for group in groups[:0:-1]:
        x = jnp.concatenate([x] + [partner(x, axis, m << group[0]) for m in range(1, 1 << len(group))], axis=1)
    if not groups:
        return [x]
    return [x] + [partner(x, axis, m << groups[0][0]) for m in range(1, 1 << len(groups[0]))]


def relative_block(owner, me, groups):
    rel = owner ^ me
    place = jnp.zeros_like(rel)
    for group in groups:
        place = (place << len(group)) | (rel >> group[0] & ((1 << len(group)) - 1))
    return place


def tied(*values):
    return lax.optimization_barrier(values)


TILE = 256


def hot_tile(place, start, rows):
    rel = place - start
    rel = jnp.where((rel >= 0) & (rel < rows), rel, -1).astype(F32).astype(BF16)
    row = lax.broadcasted_iota(jnp.int32, (rows, place.shape[1]), 0).astype(F32).astype(BF16)
    return jnp.where(row == rel, jnp.ones((), BF16), jnp.zeros((), BF16))


def pick_kernel(*refs):
    pieces, (place_ref, block_ref, out_ref) = refs[:-3], refs[-3:]

    @pl.when(pl.program_id(0) == 0)
    def _():
        out_ref[...] = jnp.zeros_like(out_ref)

    place = place_ref[...]
    picked = jnp.zeros((out_ref.shape[0], place.shape[1]), F32)
    start = 0
    for piece in pieces:
        width = piece.shape[1]
        tile = min(TILE, width)
        for k in range(0, width, tile):
            picked += dot(piece[:, k : k + tile], hot_tile(place, start + k, tile))
        start += width
    out_ref[...] += dot(picked.astype(BF16), block_ref[...])


def picked_product(pieces, place, block):
    if pieces[0].shape[1] % TILE:
        pieces = [jnp.concatenate(pieces, axis=1)]
    rows, count, width = pieces[0].shape[0], place.shape[0], block.shape[1]
    step = min(count, 1024)
    extent = sum(p.shape[1] for p in pieces)
    return pl.pallas_call(
        pick_kernel,
        grid=(count // step,),
        in_specs=[pl.BlockSpec(p.shape, lambda i: (0, 0)) for p in pieces]
        + [pl.BlockSpec((1, step), lambda i: (0, i)), pl.BlockSpec((step, width), lambda i: (i, 0))],
        out_specs=pl.BlockSpec((rows, width), lambda i: (0, 0)),
        out_shape=jax.ShapeDtypeStruct((rows, width), F32),
        compiler_params=pltpu.CompilerParams(vmem_limit_bytes=16 << 20),
        cost_estimate=pl.CostEstimate(
            flops=2 * rows * count * (extent + width), bytes_accessed=2 * count * (width + 2 * extent), transcendentals=0
        ),
    )(*pieces, place[None, :], block)


def put_kernel(update_ref, place_ref, out_ref, *, first):
    update, place = update_ref[...], place_ref[...]
    width = out_ref.shape[1]
    tile = min(TILE, width)
    for n in range(0, width, tile):
        hot = hot_tile(place, first + n, tile)
        total = lax.dot_general(update, hot, (((1,), (1,)), ((), ())), preferred_element_type=F32)
        out_ref[:, n : n + tile] = total.astype(out_ref.dtype)


def put_columns(update, place, first, width, dtype):
    rows, count = update.shape
    return pl.pallas_call(
        functools.partial(put_kernel, first=first),
        out_shape=jax.ShapeDtypeStruct((rows, width), dtype),
        compiler_params=pltpu.CompilerParams(vmem_limit_bytes=16 << 20),
        cost_estimate=pl.CostEstimate(flops=2 * rows * count * width, bytes_accessed=4 * rows * width, transcendentals=0),
    )(update, place)


def join_kernel(core_ref, own_ref, other_ref, out_ref):
    mine = pl.program_id(0) == core_ref[0]

    @pl.when(mine)
    def _():
        out_ref[...] = own_ref[...]

    @pl.when(jnp.logical_not(mine))
    def _():
        out_ref[...] = other_ref[...]


def join(own, other, core):
    rows, width = own.shape
    if width % 128:
        return jnp.concatenate([jnp.where(core == 0, own, other), jnp.where(core == 0, other, own)], axis=1)
    return pl.pallas_call(
        join_kernel,
        grid_spec=pltpu.PrefetchScalarGridSpec(
            num_scalar_prefetch=1,
            grid=(2,),
            in_specs=[pl.BlockSpec((rows, width), lambda i, core: (0, 0))] * 2,
            out_specs=pl.BlockSpec((rows, width), lambda i, core: (0, i)),
        ),
        out_shape=jax.ShapeDtypeStruct((rows, 2 * width), own.dtype),
        compiler_params=pltpu.CompilerParams(vmem_limit_bytes=16 << 20),
        cost_estimate=pl.CostEstimate(flops=0, bytes_accessed=4 * own.size * own.dtype.itemsize, transcendentals=0),
    )(core[None], own, other)


def per_device(
    rhs_zero, rhs_one, rhs_two,
    pivot_zero, pivot_one, pivot_two,
    lower_one, lower_two,
    upper_one, upper_two,
    back_zero, back_one, back_two,
    index_one, index_two,
):
    sep = lower_one.shape[0] * lax.axis_size("front")
    leaves = lax.axis_size("leaf")
    me = lax.axis_index("leaf")
    front_pos = lax.axis_index("front")
    core = front_pos & 1
    leaf_bits = leaves.bit_length() - 1
    front_bits = lax.axis_size("front").bit_length() - 1
    groups = [bit_groups(range(leaf_bits - level)) for level in range(3)]
    away = bit_groups(range(1, front_bits))

    def own_index(level):
        table = index_one if level == 1 else index_two
        width = leaves >> level
        chunk = table.shape[1] // width
        start = (me & width - 1) * chunk
        entries = lax.dynamic_slice(table, (me >> (leaf_bits - level), start), (1, chunk))[0]
        return entries

    def split_place(column, level):
        block = sep // (leaves >> level)
        half = block // 2
        owner = column // block
        mine = me & (leaves >> level) - 1
        rel = relative_block(owner, mine, groups[level])
        return ((column // half & 1) ^ core) * (sep // 2) + rel * half + column % half

    def half_of(x, which, dim):
        size = x.shape[dim] // 2
        return lax.dynamic_slice_in_dim(x, which * size, size, dim)

    def own_half(x):
        width = x.shape[1] // 2
        return jnp.where(core == 0, x[:, :width], x[:, width:])

    def row_total(keep, send, level):
        return scatter_sum(keep + partner(send, "front", 1).astype(F32), "leaf", groups[level])

    def put_halves(update, place):
        send = put_columns(update, place, sep // 2, sep // 2, BF16)
        return put_columns(update, place, 0, sep // 2, F32), send

    def halves(w):
        return half_of(w, core, 1), half_of(w, 1 - core, 1)

    def front_half(x, split):
        keep, send = split
        other = partner(dot(x, send), "front", 1)
        return exchange_sum(dot(x, keep) + other, "front", away)

    def outputs(own):
        return join(own, partner(own, "front", 1), core)

    def in_order(own, other):
        return jnp.concatenate([jnp.where(core == 0, own, other), jnp.where(core == 0, other, own)], axis=1)

    def both_halves(own):
        return in_order(own, partner(own, "front", 1))

    def known_pieces(half, within):
        own = gather_blocks(half.astype(BF16), "leaf", within)
        return own + [partner(piece, "front", 1) for piece in own]

    index = own_index(2)
    is_root = index < sep
    place_one = jnp.where(is_root, -1, split_place(index - sep, 1))
    place_root = jnp.where(is_root, split_place(index, 0), -1)
    place_up = split_place(own_index(1), 0)
    put_one, put_root, put_up = tied(*(half_of(p, core, 0)[None, :] for p in (place_one, place_root, place_up)))
    y_two = exchange_sum(dot(rhs_two.astype(BF16), pivot_two), "leaf", groups[2])
    y_two, keep, send = tied(y_two, *halves(lower_two))
    low = y_two.astype(BF16)
    other = partner(dot(low, send), "front", 1)
    total = dot(low, keep) + other
    update = exchange_sum(total, "front", away).astype(BF16)
    update, rhs_half = tied(update, own_half(rhs_one))
    keep, send = put_halves(update, put_one)

    half = (rhs_half - row_total(keep, send, 1)).astype(BF16)
    y_one = exchange_sum(dot(both_halves(half), pivot_one), "leaf", groups[1])
    y_one, root_keep, root_send, keep, send = tied(y_one, *put_halves(update, put_root), *halves(lower_one))
    low = y_one.astype(BF16)
    total = partner(dot(low, send), "front", 1)
    total = dot(low, keep) + total
    update = exchange_sum(total, "front", away).astype(BF16)
    update, rhs_half = tied(update, own_half(rhs_zero))
    keep, send = put_halves(update, put_up)
    keep, send = root_keep + keep, root_send + send

    near, far = groups[0][:1], groups[0][1:]
    count = 1 << len(near[0])
    block = pivot_zero.shape[1] // count
    starts = [((me & count - 1) ^ m) * block for m in range(count)]
    pivot_rel = jnp.concatenate([lax.dynamic_slice_in_dim(pivot_zero, at, block, 1) for at in starts], axis=1)
    back_rel = jnp.concatenate([lax.dynamic_slice_in_dim(back_zero, at, block, 0) for at in starts], axis=0)
    half = (rhs_half - row_total(keep, send, 0)).astype(BF16)
    half, pivot_rel, keep, send = tied(half, pivot_rel, *halves(back_rel))
    y_zero = exchange_sum(scatter_sum(dot(both_halves(half), pivot_rel), "leaf", near), "leaf", far)
    y_zero = jnp.concatenate(gather_blocks(y_zero.astype(BF16), "leaf", near), axis=1)
    y_zero, *split_one = tied(y_zero, *halves(back_one))
    x_zero = front_half(y_zero, (keep, send))
    known_zero = known_pieces(x_zero, groups[0])

    coupling = exchange_sum(picked_product(known_zero, place_up, upper_one), "leaf", groups[1])
    coupling, coupling_root = tied(coupling, picked_product(known_zero, place_root, upper_two))
    z_one = y_one - coupling
    x_one = front_half(z_one.astype(BF16), split_one)
    x_one, x_zero = tied(x_one, x_zero)
    known_one = known_pieces(x_one, groups[1])
    *known_one, solution_zero, keep, send = tied(*known_one, outputs(x_zero), *halves(back_two))

    coupling = coupling_root + picked_product(known_one, place_one, upper_two)
    coupling, x_one = tied(coupling, x_one)
    coupling, solution_one = tied(exchange_sum(coupling, "leaf", groups[2]), outputs(x_one))
    x_two = front_half((y_two - coupling).astype(BF16), (keep, send))
    return solution_zero, solution_one, outputs(x_two)


def solution(mesh):
    by_leaf = P(None, "leaf")
    rows = P("leaf", "front")
    columns = P("front", "leaf")
    return jax.shard_map(
        per_device,
        mesh=mesh,
        in_specs=(by_leaf,) * 3 + (rows,) * 3 + (columns,) * 2 + (rows,) * 2 + (columns,) * 3 + (P(), P()),
        out_specs=(by_leaf,) * 3,
        check_vma=False,
    )
```

```python
import functools

import jax
import jax.numpy as jnp
from jax import lax
from jax.experimental import pallas as pl
from jax.experimental.pallas import tpu as pltpu
from jax.sharding import PartitionSpec as P

BF16 = jnp.bfloat16
F32 = jnp.float32


def dot(left, right):
    return jnp.dot(left, right, preferred_element_type=F32)


def bit_groups(bits):
    bits = list(bits)
    return [bits[i : i + 2] for i in range(0, len(bits), 2)]


def partner(x, axis, mask):
    return lax.ppermute(x, axis, [(i, i ^ mask) for i in range(lax.axis_size(axis))])


def exchange_sum(x, axis, groups):
    for group in groups:
        low = x.astype(BF16)
        parts = [low] + [partner(low, axis, m << group[0]) for m in range(1, 1 << len(group))]
        parts = [p.astype(F32) for p in parts]
        while len(parts) > 1:
            parts = [parts[i] + parts[i + 1] for i in range(0, len(parts), 2)]
        x = parts[0]
    return x


def scatter_sum(x, axis, groups):
    for group in groups:
        count = 1 << len(group)
        width = x.shape[1] // count
        total = x[:, :width]
        for m in range(1, count):
            piece = x[:, m * width : (m + 1) * width].astype(BF16)
            total = total + partner(piece, axis, m << group[0]).astype(F32)
        x = total
    return x


def gather_blocks(x, axis, groups):
    for group in groups[:0:-1]:
        x = jnp.concatenate([x] + [partner(x, axis, m << group[0]) for m in range(1, 1 << len(group))], axis=1)
    if not groups:
        return [x]
    return [x] + [partner(x, axis, m << groups[0][0]) for m in range(1, 1 << len(groups[0]))]


def relative_block(owner, me, groups):
    rel = owner ^ me
    place = jnp.zeros_like(rel)
    for group in groups:
        place = (place << len(group)) | (rel >> group[0] & ((1 << len(group)) - 1))
    return place


def tied(*values):
    return lax.optimization_barrier(values)


TILE = 256


def hot_tile(place, start, rows):
    rel = place - start
    rel = jnp.where((rel >= 0) & (rel < rows), rel, -1).astype(F32).astype(BF16)
    row = lax.broadcasted_iota(jnp.int32, (rows, place.shape[1]), 0).astype(F32).astype(BF16)
    return jnp.where(row == rel, jnp.ones((), BF16), jnp.zeros((), BF16))


def pick_kernel(*refs):
    pieces, (place_ref, block_ref, out_ref) = refs[:-3], refs[-3:]

    @pl.when(pl.program_id(0) == 0)
    def _():
        out_ref[...] = jnp.zeros_like(out_ref)

    place = place_ref[...]
    picked = jnp.zeros((out_ref.shape[0], place.shape[1]), F32)
    start = 0
    for piece in pieces:
        width = piece.shape[1]
        tile = min(TILE, width)
        for k in range(0, width, tile):
            picked += dot(piece[:, k : k + tile], hot_tile(place, start + k, tile))
        start += width
    out_ref[...] += dot(picked.astype(BF16), block_ref[...])


def picked_product(pieces, place, block):
    if pieces[0].shape[1] % TILE:
        pieces = [jnp.concatenate(pieces, axis=1)]
    rows, count, width = pieces[0].shape[0], place.shape[0], block.shape[1]
    step = min(count, 1024)
    extent = sum(p.shape[1] for p in pieces)
    return pl.pallas_call(
        pick_kernel,
        grid=(count // step,),
        in_specs=[pl.BlockSpec(p.shape, lambda i: (0, 0)) for p in pieces]
        + [pl.BlockSpec((1, step), lambda i: (0, i)), pl.BlockSpec((step, width), lambda i: (i, 0))],
        out_specs=pl.BlockSpec((rows, width), lambda i: (0, 0)),
        out_shape=jax.ShapeDtypeStruct((rows, width), F32),
        compiler_params=pltpu.CompilerParams(vmem_limit_bytes=12 << 20),
        cost_estimate=pl.CostEstimate(
            flops=2 * rows * count * (extent + width), bytes_accessed=2 * count * (width + 2 * extent), transcendentals=0
        ),
    )(*pieces, place[None, :], block)


def put_kernel(update_ref, place_ref, out_ref, *, first):
    update, place = update_ref[...], place_ref[...]
    width = out_ref.shape[1]
    tile = min(TILE, width)
    for n in range(0, width, tile):
        hot = hot_tile(place, first + n, tile)
        total = lax.dot_general(update, hot, (((1,), (1,)), ((), ())), preferred_element_type=F32)
        out_ref[:, n : n + tile] = total.astype(out_ref.dtype)


def put_columns(update, place, first, width, dtype):
    rows, count = update.shape
    return pl.pallas_call(
        functools.partial(put_kernel, first=first),
        out_shape=jax.ShapeDtypeStruct((rows, width), dtype),
        compiler_params=pltpu.CompilerParams(vmem_limit_bytes=6 << 20),
        cost_estimate=pl.CostEstimate(flops=2 * rows * count * width, bytes_accessed=4 * rows * width, transcendentals=0),
    )(update, place)


def join_kernel(core_ref, own_ref, other_ref, out_ref):
    mine = pl.program_id(0) == core_ref[0]

    @pl.when(mine)
    def _():
        out_ref[...] = own_ref[...]

    @pl.when(jnp.logical_not(mine))
    def _():
        out_ref[...] = other_ref[...]


def join(own, other, core):
    rows, width = own.shape
    if width % 128:
        return jnp.concatenate([jnp.where(core == 0, own, other), jnp.where(core == 0, other, own)], axis=1)
    return pl.pallas_call(
        join_kernel,
        grid_spec=pltpu.PrefetchScalarGridSpec(
            num_scalar_prefetch=1,
            grid=(2,),
            in_specs=[pl.BlockSpec((rows, width), lambda i, core: (0, 0))] * 2,
            out_specs=pl.BlockSpec((rows, width), lambda i, core: (0, i)),
        ),
        out_shape=jax.ShapeDtypeStruct((rows, 2 * width), own.dtype),
        compiler_params=pltpu.CompilerParams(vmem_limit_bytes=4 << 20),
        cost_estimate=pl.CostEstimate(flops=0, bytes_accessed=32 * own.size * own.dtype.itemsize, transcendentals=0),
    )(core[None], own, other)


def per_device(
    rhs_zero, rhs_one, rhs_two,
    pivot_zero, pivot_one, pivot_two,
    lower_one, lower_two,
    upper_one, upper_two,
    back_zero, back_one, back_two,
    index_one, index_two,
):
    sep = lower_one.shape[0] * lax.axis_size("front")
    leaves = lax.axis_size("leaf")
    me = lax.axis_index("leaf")
    front_pos = lax.axis_index("front")
    core = front_pos & 1
    leaf_bits = leaves.bit_length() - 1
    front_bits = lax.axis_size("front").bit_length() - 1
    groups = [bit_groups(range(leaf_bits - level)) for level in range(3)]
    away = bit_groups(range(1, front_bits))

    def own_index(level):
        table = index_one if level == 1 else index_two
        width = leaves >> level
        chunk = table.shape[1] // width
        start = (me & width - 1) * chunk
        entries = lax.dynamic_slice(table, (me >> (leaf_bits - level), start), (1, chunk))[0]
        return entries

    def split_place(column, level):
        block = sep // (leaves >> level)
        half = block // 2
        owner = column // block
        mine = me & (leaves >> level) - 1
        rel = relative_block(owner, mine, groups[level])
        return ((column // half & 1) ^ core) * (sep // 2) + rel * half + column % half

    def half_of(x, which, dim):
        size = x.shape[dim] // 2
        return lax.dynamic_slice_in_dim(x, which * size, size, dim)

    def own_half(x):
        width = x.shape[1] // 2
        return jnp.where(core == 0, x[:, :width], x[:, width:])

    def row_total(keep, send, level):
        return scatter_sum(keep + partner(send, "front", 1).astype(F32), "leaf", groups[level])

    def put_halves(update, place):
        send = put_columns(update, place, sep // 2, sep // 2, BF16)
        return put_columns(update, place, 0, sep // 2, F32), send

    def halves(w):
        return half_of(w, core, 1), half_of(w, 1 - core, 1)

    def front_half(x, split):
        keep, send = split
        other = partner(dot(x, send), "front", 1)
        return exchange_sum(dot(x, keep) + other, "front", away)

    def outputs(own):
        return join(own, partner(own, "front", 1), core)

    def in_order(own, other):
        return jnp.concatenate([jnp.where(core == 0, own, other), jnp.where(core == 0, other, own)], axis=1)

    def both_halves(own):
        return in_order(own, partner(own, "front", 1))

    def known_pieces(half, within):
        own = gather_blocks(half.astype(BF16), "leaf", within)
        return own + [partner(piece, "front", 1) for piece in own]

    index = own_index(2)
    is_root = index < sep
    place_one = jnp.where(is_root, -1, split_place(index - sep, 1))
    place_root = jnp.where(is_root, split_place(index, 0), -1)
    place_up = split_place(own_index(1), 0)
    put_one, put_root, put_up = tied(*(half_of(p, core, 0)[None, :] for p in (place_one, place_root, place_up)))
    y_two = exchange_sum(dot(rhs_two.astype(BF16), pivot_two), "leaf", groups[2]).astype(BF16)
    y_two, keep, send = tied(y_two, *halves(lower_two))
    low = y_two.astype(BF16)
    other = partner(dot(low, send), "front", 1)
    total, other = tied(dot(low, keep), other)
    total = total + other
    update = exchange_sum(total, "front", away).astype(BF16)
    update, rhs_half = tied(update, own_half(rhs_one))
    keep, send = put_halves(update, put_one)

    half = (rhs_half - row_total(keep, send, 1)).astype(BF16)
    y_one = exchange_sum(dot(both_halves(half), pivot_one), "leaf", groups[1]).astype(BF16)
    y_one, root_keep, root_send, keep, send = tied(y_one, *put_halves(update, put_root), *halves(lower_one))
    low = y_one.astype(BF16)
    total = partner(dot(low, send), "front", 1)
    total = dot(low, keep) + total
    update = exchange_sum(total, "front", away).astype(BF16)
    update, rhs_half = tied(update, own_half(rhs_zero))
    keep, send = put_halves(update, put_up)
    keep, send = root_keep + keep, root_send + send

    near, far = groups[0][:1], groups[0][1:]
    count = 1 << len(near[0])
    block = pivot_zero.shape[1] // count
    starts = [((me & count - 1) ^ m) * block for m in range(count)]
    pivot_rel = jnp.concatenate([lax.dynamic_slice_in_dim(pivot_zero, at, block, 1) for at in starts], axis=1)
    back_rel = jnp.concatenate([lax.dynamic_slice_in_dim(back_zero, at, block, 0) for at in starts], axis=0)
    half = (rhs_half - row_total(keep, send, 0)).astype(BF16)
    half, pivot_rel, keep, send = tied(half, pivot_rel, *halves(back_rel))
    y_zero = exchange_sum(scatter_sum(dot(both_halves(half), pivot_rel), "leaf", near), "leaf", far)
    y_zero = jnp.concatenate(gather_blocks(y_zero.astype(BF16), "leaf", near), axis=1)
    y_zero, *split_one = tied(y_zero, *halves(back_one))
    x_zero = front_half(y_zero, (keep, send))
    known_zero = known_pieces(x_zero, groups[0])

    coupling = exchange_sum(picked_product(known_zero, place_up, upper_one), "leaf", groups[1])
    coupling, coupling_root = tied(coupling, picked_product(known_zero, place_root, upper_two))
    z_one = y_one - coupling
    z_one, x_zero = tied(z_one.astype(BF16), x_zero)
    x_one, solution_zero = tied(front_half(z_one, split_one), outputs(x_zero))
    known_one = known_pieces(x_one, groups[1])
    *known_one, keep, send = tied(*known_one, *halves(back_two))

    coupling = coupling_root + picked_product(known_one, place_one, upper_two)
    coupling, other = tied(coupling, partner(x_one, "front", 1))
    coupling, solution_one = tied(exchange_sum(coupling, "leaf", groups[2]), join(x_one, other, core))
    x_two = front_half((y_two - coupling).astype(BF16), (keep, send))
    return solution_zero, solution_one, outputs(x_two)


def solution(mesh):
    by_leaf = P(None, "leaf")
    rows = P("leaf", "front")
    columns = P("front", "leaf")
    return jax.shard_map(
        per_device,
        mesh=mesh,
        in_specs=(by_leaf,) * 3 + (rows,) * 3 + (columns,) * 2 + (rows,) * 2 + (columns,) * 3 + (P(), P()),
        out_specs=(by_leaf,) * 3,
        check_vma=False,
    )
```

```python
import functools

import jax
import jax.numpy as jnp
from jax import lax
from jax.experimental import pallas as pl
from jax.experimental.pallas import tpu as pltpu
from jax.sharding import PartitionSpec as P

BF16 = jnp.bfloat16
F32 = jnp.float32


def dot(left, right):
    return jnp.dot(left, right, preferred_element_type=F32)


def bit_groups(bits):
    bits = list(bits)
    return [bits[i : i + 2] for i in range(0, len(bits), 2)]


def partner(x, axis, mask):
    return lax.ppermute(x, axis, [(i, i ^ mask) for i in range(lax.axis_size(axis))])


def exchange_sum(x, axis, groups):
    for group in groups:
        low = x.astype(BF16)
        parts = [low] + [partner(low, axis, m << group[0]) for m in range(1, 1 << len(group))]
        parts = [p.astype(F32) for p in parts]
        while len(parts) > 1:
            parts = [parts[i] + parts[i + 1] for i in range(0, len(parts), 2)]
        x = parts[0]
    return x


def scatter_sum(x, axis, groups):
    for group in groups:
        count = 1 << len(group)
        width = x.shape[1] // count
        total = x[:, :width]
        for m in range(1, count):
            piece = x[:, m * width : (m + 1) * width].astype(BF16)
            total = total + partner(piece, axis, m << group[0]).astype(F32)
        x = total
    return x


def gather_blocks(x, axis, groups):
    for group in groups[:0:-1]:
        x = jnp.concatenate([x] + [partner(x, axis, m << group[0]) for m in range(1, 1 << len(group))], axis=1)
    if not groups:
        return [x]
    return [x] + [partner(x, axis, m << groups[0][0]) for m in range(1, 1 << len(groups[0]))]


def relative_block(owner, me, groups):
    rel = owner ^ me
    place = jnp.zeros_like(rel)
    for group in groups:
        place = (place << len(group)) | (rel >> group[0] & ((1 << len(group)) - 1))
    return place


def tied(*values):
    return lax.optimization_barrier(values)


TILE = 256


def hot_tile(place, start, rows):
    rel = place - start
    rel = jnp.where((rel >= 0) & (rel < rows), rel, -1).astype(F32).astype(BF16)
    row = lax.broadcasted_iota(jnp.int32, (rows, place.shape[1]), 0).astype(F32).astype(BF16)
    return jnp.where(row == rel, jnp.ones((), BF16), jnp.zeros((), BF16))


def pick_kernel(*refs):
    pieces, (place_ref, block_ref, out_ref) = refs[:-3], refs[-3:]

    @pl.when(pl.program_id(0) == 0)
    def _():
        out_ref[...] = jnp.zeros_like(out_ref)

    place = place_ref[...]
    picked = jnp.zeros((out_ref.shape[0], place.shape[1]), F32)
    start = 0
    for piece in pieces:
        width = piece.shape[1]
        tile = min(TILE, width)
        for k in range(0, width, tile):
            picked += dot(piece[:, k : k + tile], hot_tile(place, start + k, tile))
        start += width
    out_ref[...] += dot(picked.astype(BF16), block_ref[...])


def picked_product(pieces, place, block):
    if pieces[0].shape[1] % TILE:
        pieces = [jnp.concatenate(pieces, axis=1)]
    rows, count, width = pieces[0].shape[0], place.shape[0], block.shape[1]
    step = min(count, 1024)
    extent = sum(p.shape[1] for p in pieces)
    return pl.pallas_call(
        pick_kernel,
        grid=(count // step,),
        in_specs=[pl.BlockSpec(p.shape, lambda i: (0, 0)) for p in pieces]
        + [pl.BlockSpec((1, step), lambda i: (0, i)), pl.BlockSpec((step, width), lambda i: (i, 0))],
        out_specs=pl.BlockSpec((rows, width), lambda i: (0, 0)),
        out_shape=jax.ShapeDtypeStruct((rows, width), F32),
        compiler_params=pltpu.CompilerParams(vmem_limit_bytes=12 << 20),
        cost_estimate=pl.CostEstimate(
            flops=2 * rows * count * (extent + width), bytes_accessed=2 * count * (width + 2 * extent), transcendentals=0
        ),
    )(*pieces, place[None, :], block)


def put_kernel(update_ref, place_ref, out_ref, *, first):
    update, place = update_ref[...], place_ref[...]
    width = out_ref.shape[1]
    tile = min(TILE, width)
    for n in range(0, width, tile):
        hot = hot_tile(place, first + n, tile)
        total = lax.dot_general(update, hot, (((1,), (1,)), ((), ())), preferred_element_type=F32)
        out_ref[:, n : n + tile] = total.astype(out_ref.dtype)


def put_columns(update, place, first, width, dtype):
    rows, count = update.shape
    return pl.pallas_call(
        functools.partial(put_kernel, first=first),
        out_shape=jax.ShapeDtypeStruct((rows, width), dtype),
        compiler_params=pltpu.CompilerParams(vmem_limit_bytes=6 << 20),
        cost_estimate=pl.CostEstimate(flops=2 * rows * count * width, bytes_accessed=4 * rows * width, transcendentals=0),
    )(update, place)


def join_kernel(core_ref, own_ref, other_ref, out_ref):
    mine = pl.program_id(0) == core_ref[0]

    @pl.when(mine)
    def _():
        out_ref[...] = own_ref[...]

    @pl.when(jnp.logical_not(mine))
    def _():
        out_ref[...] = other_ref[...]


def join(own, other, core):
    rows, width = own.shape
    if width % 128:
        return jnp.concatenate([jnp.where(core == 0, own, other), jnp.where(core == 0, other, own)], axis=1)
    return pl.pallas_call(
        join_kernel,
        grid_spec=pltpu.PrefetchScalarGridSpec(
            num_scalar_prefetch=1,
            grid=(2,),
            in_specs=[pl.BlockSpec((rows, width), lambda i, core: (0, 0))] * 2,
            out_specs=pl.BlockSpec((rows, width), lambda i, core: (0, i)),
        ),
        out_shape=jax.ShapeDtypeStruct((rows, 2 * width), own.dtype),
        compiler_params=pltpu.CompilerParams(vmem_limit_bytes=4 << 20),
        cost_estimate=pl.CostEstimate(flops=0, bytes_accessed=32 * own.size * own.dtype.itemsize, transcendentals=0),
    )(core[None], own, other)


def per_device(
    rhs_zero, rhs_one, rhs_two,
    pivot_zero, pivot_one, pivot_two,
    lower_one, lower_two,
    upper_one, upper_two,
    back_zero, back_one, back_two,
    index_one, index_two,
):
    sep = lower_one.shape[0] * lax.axis_size("front")
    leaves = lax.axis_size("leaf")
    me = lax.axis_index("leaf")
    front_pos = lax.axis_index("front")
    core = front_pos & 1
    leaf_bits = leaves.bit_length() - 1
    front_bits = lax.axis_size("front").bit_length() - 1
    groups = [bit_groups(range(leaf_bits - level)) for level in range(3)]
    away = bit_groups(range(1, front_bits))

    def own_index(level):
        table = index_one if level == 1 else index_two
        width = leaves >> level
        chunk = table.shape[1] // width
        start = (me & width - 1) * chunk
        entries = lax.dynamic_slice(table, (me >> (leaf_bits - level), start), (1, chunk))[0]
        return entries

    def split_place(column, level):
        block = sep // (leaves >> level)
        half = block // 2
        owner = column // block
        mine = me & (leaves >> level) - 1
        rel = relative_block(owner, mine, groups[level])
        return ((column // half & 1) ^ core) * (sep // 2) + rel * half + column % half

    def half_of(x, which, dim):
        size = x.shape[dim] // 2
        return lax.dynamic_slice_in_dim(x, which * size, size, dim)

    def own_half(x):
        width = x.shape[1] // 2
        return jnp.where(core == 0, x[:, :width], x[:, width:])

    def row_total(keep, send, level):
        return scatter_sum(keep + partner(send, "front", 1).astype(F32), "leaf", groups[level])

    def put_halves(update, place):
        send = put_columns(update, place, sep // 2, sep // 2, BF16)
        return put_columns(update, place, 0, sep // 2, F32), send

    def halves(w):
        return half_of(w, core, 1), half_of(w, 1 - core, 1)

    def front_half(x, split):
        keep, send = split
        other = partner(dot(x, send), "front", 1)
        return exchange_sum(dot(x, keep) + other, "front", away)

    def front_half_at_once(x, split):
        if len(away) != 1:
            return front_half(x, split)
        keep, send = split
        own, given = dot(x, keep).astype(BF16), dot(x, send).astype(BF16)
        terms = []
        for m in range(1 << len(away[0])):
            terms.append(own if m == 0 else partner(own, "front", m << 1))
            terms.append(partner(given, "front", m << 1 | 1))
        terms = [t.astype(F32) for t in terms]
        while len(terms) > 1:
            terms = [terms[i] + terms[i + 1] for i in range(0, len(terms), 2)]
        return terms[0]

    def outputs(own):
        return join(own, partner(own, "front", 1), core)

    def in_order(own, other):
        return jnp.concatenate([jnp.where(core == 0, own, other), jnp.where(core == 0, other, own)], axis=1)

    def both_halves(own):
        return in_order(own, partner(own, "front", 1))

    def known_pieces(half, within):
        own = gather_blocks(half.astype(BF16), "leaf", within)
        return own + [partner(piece, "front", 1) for piece in own]

    index = own_index(2)
    is_root = index < sep
    place_one = jnp.where(is_root, -1, split_place(index - sep, 1))
    place_root = jnp.where(is_root, split_place(index, 0), -1)
    place_up = split_place(own_index(1), 0)
    put_one, put_root, put_up = tied(*(half_of(p, core, 0)[None, :] for p in (place_one, place_root, place_up)))
    y_two = exchange_sum(dot(rhs_two.astype(BF16), pivot_two), "leaf", groups[2]).astype(BF16)
    y_two, keep, send = tied(y_two, *halves(lower_two))
    low = y_two.astype(BF16)
    other = partner(dot(low, send), "front", 1)
    total, other = tied(dot(low, keep), other)
    total = total + other
    update = exchange_sum(total, "front", away).astype(BF16)
    update, rhs_half = tied(update, own_half(rhs_one))
    keep, send = put_halves(update, put_one)

    half = (rhs_half - row_total(keep, send, 1)).astype(BF16)
    y_one = exchange_sum(dot(both_halves(half), pivot_one), "leaf", groups[1]).astype(BF16)
    y_one, root_keep, root_send, keep, send = tied(y_one, *put_halves(update, put_root), *halves(lower_one))
    low = y_one.astype(BF16)
    total = partner(dot(low, send), "front", 1)
    total = dot(low, keep) + total
    update = exchange_sum(total, "front", away).astype(BF16)
    update, rhs_half = tied(update, own_half(rhs_zero))
    keep, send = put_halves(update, put_up)
    keep, send = root_keep + keep, root_send + send

    near, far = groups[0][:1], groups[0][1:]
    count = 1 << len(near[0])
    block = pivot_zero.shape[1] // count
    starts = [((me & count - 1) ^ m) * block for m in range(count)]
    pivot_rel = jnp.concatenate([lax.dynamic_slice_in_dim(pivot_zero, at, block, 1) for at in starts], axis=1)
    back_rel = jnp.concatenate([lax.dynamic_slice_in_dim(back_zero, at, block, 0) for at in starts], axis=0)
    half = (rhs_half - row_total(keep, send, 0)).astype(BF16)
    half, pivot_rel, keep, send = tied(half, pivot_rel, *halves(back_rel))
    y_zero = exchange_sum(scatter_sum(dot(both_halves(half), pivot_rel), "leaf", near), "leaf", far)
    y_zero = jnp.concatenate(gather_blocks(y_zero.astype(BF16), "leaf", near), axis=1)
    y_zero, *split_one = tied(y_zero, *halves(back_one))
    x_zero = front_half_at_once(y_zero, (keep, send))
    known_zero = known_pieces(x_zero, groups[0])

    coupling = exchange_sum(picked_product(known_zero, place_up, upper_one), "leaf", groups[1])
    coupling, coupling_root = tied(coupling, picked_product(known_zero, place_root, upper_two))
    z_one = y_one - coupling
    z_one, x_zero = tied(z_one.astype(BF16), x_zero)
    x_one, solution_zero = tied(front_half(z_one, split_one), outputs(x_zero))
    known_one = known_pieces(x_one, groups[1])
    *known_one, keep, send = tied(*known_one, *halves(back_two))

    coupling = coupling_root + picked_product(known_one, place_one, upper_two)
    coupling, other = tied(coupling, partner(x_one, "front", 1))
    coupling, solution_one = tied(exchange_sum(coupling, "leaf", groups[2]), join(x_one, other, core))
    x_two = front_half((y_two - coupling).astype(BF16), (keep, send))
    return solution_zero, solution_one, outputs(x_two)


def solution(mesh):
    by_leaf = P(None, "leaf")
    rows = P("leaf", "front")
    columns = P("front", "leaf")
    return jax.shard_map(
        per_device,
        mesh=mesh,
        in_specs=(by_leaf,) * 3 + (rows,) * 3 + (columns,) * 2 + (rows,) * 2 + (columns,) * 3 + (P(), P()),
        out_specs=(by_leaf,) * 3,
        check_vma=False,
    )
```

```python
import functools

import jax
import jax.numpy as jnp
from jax import lax
from jax.experimental import pallas as pl
from jax.experimental.pallas import tpu as pltpu
from jax.sharding import PartitionSpec as P

BF16 = jnp.bfloat16
F32 = jnp.float32


def dot(left, right):
    return jnp.dot(left, right, preferred_element_type=F32)


def bit_groups(bits):
    bits = list(bits)
    return [bits[i : i + 2] for i in range(0, len(bits), 2)]


def partner(x, axis, mask):
    return lax.ppermute(x, axis, [(i, i ^ mask) for i in range(lax.axis_size(axis))])


def exchange_sum(x, axis, groups):
    for group in groups:
        low = x.astype(BF16)
        parts = [low] + [partner(low, axis, m << group[0]) for m in range(1, 1 << len(group))]
        parts = [p.astype(F32) for p in parts]
        while len(parts) > 1:
            parts = [parts[i] + parts[i + 1] for i in range(0, len(parts), 2)]
        x = parts[0]
    return x


def scatter_sum(x, axis, groups):
    for group in groups:
        count = 1 << len(group)
        width = x.shape[1] // count
        total = x[:, :width]
        for m in range(1, count):
            piece = x[:, m * width : (m + 1) * width].astype(BF16)
            total = total + partner(piece, axis, m << group[0]).astype(F32)
        x = total
    return x


def gather_blocks(x, axis, groups):
    for group in groups[:0:-1]:
        x = jnp.concatenate([x] + [partner(x, axis, m << group[0]) for m in range(1, 1 << len(group))], axis=1)
    if not groups:
        return [x]
    return [x] + [partner(x, axis, m << groups[0][0]) for m in range(1, 1 << len(groups[0]))]


def relative_block(owner, me, groups):
    rel = owner ^ me
    place = jnp.zeros_like(rel)
    for group in groups:
        place = (place << len(group)) | (rel >> group[0] & ((1 << len(group)) - 1))
    return place


def tied(*values):
    return lax.optimization_barrier(values)


TILE = 256


def hot_tile(place, start, rows):
    rel = place - start
    rel = jnp.where((rel >= 0) & (rel < rows), rel, -1).astype(F32).astype(BF16)
    row = lax.broadcasted_iota(jnp.int32, (rows, place.shape[1]), 0).astype(F32).astype(BF16)
    return jnp.where(row == rel, jnp.ones((), BF16), jnp.zeros((), BF16))


def pick_kernel(*refs):
    pieces, (place_ref, block_ref, out_ref) = refs[:-3], refs[-3:]

    @pl.when(pl.program_id(0) == 0)
    def _():
        out_ref[...] = jnp.zeros_like(out_ref)

    place = place_ref[...]
    picked = jnp.zeros((out_ref.shape[0], place.shape[1]), F32)
    start = 0
    for piece in pieces:
        width = piece.shape[1]
        tile = min(TILE, width)
        for k in range(0, width, tile):
            picked += dot(piece[:, k : k + tile], hot_tile(place, start + k, tile))
        start += width
    out_ref[...] += dot(picked.astype(BF16), block_ref[...])


def picked_product(pieces, place, block):
    if pieces[0].shape[1] % TILE:
        pieces = [jnp.concatenate(pieces, axis=1)]
    rows, count, width = pieces[0].shape[0], place.shape[0], block.shape[1]
    step = min(count, 1024)
    extent = sum(p.shape[1] for p in pieces)
    return pl.pallas_call(
        pick_kernel,
        grid=(count // step,),
        in_specs=[pl.BlockSpec(p.shape, lambda i: (0, 0)) for p in pieces]
        + [pl.BlockSpec((1, step), lambda i: (0, i)), pl.BlockSpec((step, width), lambda i: (i, 0))],
        out_specs=pl.BlockSpec((rows, width), lambda i: (0, 0)),
        out_shape=jax.ShapeDtypeStruct((rows, width), F32),
        compiler_params=pltpu.CompilerParams(vmem_limit_bytes=12 << 20),
        cost_estimate=pl.CostEstimate(
            flops=2 * rows * count * (extent + width), bytes_accessed=2 * count * (width + 2 * extent), transcendentals=0
        ),
    )(*pieces, place[None, :], block)


def put_kernel(update_ref, place_ref, out_ref, *, first):
    update, place = update_ref[...], place_ref[...]
    width = out_ref.shape[1]
    tile = min(TILE, width)
    for n in range(0, width, tile):
        hot = hot_tile(place, first + n, tile)
        total = lax.dot_general(update, hot, (((1,), (1,)), ((), ())), preferred_element_type=F32)
        out_ref[:, n : n + tile] = total.astype(out_ref.dtype)


def put_columns(update, place, first, width, dtype):
    rows, count = update.shape
    return pl.pallas_call(
        functools.partial(put_kernel, first=first),
        out_shape=jax.ShapeDtypeStruct((rows, width), dtype),
        compiler_params=pltpu.CompilerParams(vmem_limit_bytes=6 << 20),
        cost_estimate=pl.CostEstimate(flops=2 * rows * count * width, bytes_accessed=4 * rows * width, transcendentals=0),
    )(update, place)


def join_kernel(core_ref, own_ref, other_ref, out_ref):
    mine = pl.program_id(0) == core_ref[0]

    @pl.when(mine)
    def _():
        out_ref[...] = own_ref[...]

    @pl.when(jnp.logical_not(mine))
    def _():
        out_ref[...] = other_ref[...]


def join(own, other, core):
    rows, width = own.shape
    if width % 128:
        return jnp.concatenate([jnp.where(core == 0, own, other), jnp.where(core == 0, other, own)], axis=1)
    return pl.pallas_call(
        join_kernel,
        grid_spec=pltpu.PrefetchScalarGridSpec(
            num_scalar_prefetch=1,
            grid=(2,),
            in_specs=[pl.BlockSpec((rows, width), lambda i, core: (0, 0))] * 2,
            out_specs=pl.BlockSpec((rows, width), lambda i, core: (0, i)),
        ),
        out_shape=jax.ShapeDtypeStruct((rows, 2 * width), own.dtype),
        compiler_params=pltpu.CompilerParams(vmem_limit_bytes=4 << 20),
        cost_estimate=pl.CostEstimate(flops=0, bytes_accessed=32 * own.size * own.dtype.itemsize, transcendentals=0),
    )(core[None], own, other)


def per_device(
    rhs_zero, rhs_one, rhs_two,
    pivot_zero, pivot_one, pivot_two,
    lower_one, lower_two,
    upper_one, upper_two,
    back_zero, back_one, back_two,
    index_one, index_two,
):
    sep = lower_one.shape[0] * lax.axis_size("front")
    leaves = lax.axis_size("leaf")
    me = lax.axis_index("leaf")
    front_pos = lax.axis_index("front")
    core = front_pos & 1
    leaf_bits = leaves.bit_length() - 1
    front_bits = lax.axis_size("front").bit_length() - 1
    groups = [bit_groups(range(leaf_bits - level)) for level in range(3)]
    away = bit_groups(range(1, front_bits))

    def own_index(level):
        table = index_one if level == 1 else index_two
        width = leaves >> level
        chunk = table.shape[1] // width
        start = (me & width - 1) * chunk
        entries = lax.dynamic_slice(table, (me >> (leaf_bits - level), start), (1, chunk))[0]
        return entries

    def split_place(column, level):
        block = sep // (leaves >> level)
        half = block // 2
        owner = column // block
        mine = me & (leaves >> level) - 1
        rel = relative_block(owner, mine, groups[level])
        return ((column // half & 1) ^ core) * (sep // 2) + rel * half + column % half

    def half_of(x, which, dim):
        size = x.shape[dim] // 2
        return lax.dynamic_slice_in_dim(x, which * size, size, dim)

    def own_half(x):
        width = x.shape[1] // 2
        return jnp.where(core == 0, x[:, :width], x[:, width:])

    def row_total(keep, send, level):
        return scatter_sum(keep + partner(send, "front", 1).astype(F32), "leaf", groups[level])

    def put_halves(update, place):
        send = put_columns(update, place, sep // 2, sep // 2, BF16)
        return put_columns(update, place, 0, sep // 2, F32), send

    def halves(w):
        return half_of(w, core, 1), half_of(w, 1 - core, 1)

    def front_half(x, split):
        keep, send = split
        other = partner(dot(x, send), "front", 1)
        return exchange_sum(dot(x, keep) + other, "front", away)

    def front_half_at_once(x, split):
        if len(away) != 1:
            return front_half(x, split)
        keep, send = split
        own, given = dot(x, keep).astype(BF16), dot(x, send).astype(BF16)
        terms = []
        for m in range(1 << len(away[0])):
            terms.append(own if m == 0 else partner(own, "front", m << 1))
            terms.append(partner(given, "front", m << 1 | 1))
        terms = [t.astype(F32) for t in terms]
        while len(terms) > 1:
            terms = [terms[i] + terms[i + 1] for i in range(0, len(terms), 2)]
        return terms[0]

    def outputs(own):
        return join(own, partner(own, "front", 1), core)

    def in_order(own, other):
        return jnp.concatenate([jnp.where(core == 0, own, other), jnp.where(core == 0, other, own)], axis=1)

    def both_halves(own):
        return in_order(own, partner(own, "front", 1))

    def known_pieces(half, within):
        own = gather_blocks(half.astype(BF16), "leaf", within)
        return own + [partner(piece, "front", 1) for piece in own]

    index = own_index(2)
    is_root = index < sep
    place_one = jnp.where(is_root, -1, split_place(index - sep, 1))
    place_root = jnp.where(is_root, split_place(index, 0), -1)
    place_up = split_place(own_index(1), 0)
    put_one, put_root, put_up = tied(*(half_of(p, core, 0)[None, :] for p in (place_one, place_root, place_up)))
    y_two = exchange_sum(dot(rhs_two.astype(BF16), pivot_two), "leaf", groups[2]).astype(BF16)
    y_two, keep, send = tied(y_two, *halves(lower_two))
    low = y_two.astype(BF16)
    other = partner(dot(low, send), "front", 1)
    total, other = tied(dot(low, keep), other)
    total = total + other
    update = exchange_sum(total, "front", away).astype(BF16)
    update, rhs_half = tied(update, own_half(rhs_one))
    keep, send = put_halves(update, put_one)

    half = (rhs_half - row_total(keep, send, 1)).astype(BF16)
    y_one = exchange_sum(dot(both_halves(half), pivot_one), "leaf", groups[1]).astype(BF16)
    y_one, root_keep, root_send, keep, send = tied(y_one, *put_halves(update, put_root), *halves(lower_one))
    low = y_one.astype(BF16)
    total = partner(dot(low, send), "front", 1)
    total = dot(low, keep) + total
    update = exchange_sum(total, "front", away).astype(BF16)
    update, rhs_half = tied(update, own_half(rhs_zero))
    keep, send = put_halves(update, put_up)
    keep, send = root_keep + keep, root_send + send

    near, far = groups[0][:1], groups[0][1:]
    count = 1 << len(near[0])
    block = pivot_zero.shape[1] // count
    starts = [((me & count - 1) ^ m) * block for m in range(count)]
    pivot_rel = jnp.concatenate([lax.dynamic_slice_in_dim(pivot_zero, at, block, 1) for at in starts], axis=1)
    back_rel = jnp.concatenate([lax.dynamic_slice_in_dim(back_zero, at, block, 0) for at in starts], axis=0)
    half = (rhs_half - row_total(keep, send, 0)).astype(BF16)
    half, pivot_rel, keep, send = tied(half, pivot_rel, *halves(back_rel))
    y_zero = exchange_sum(scatter_sum(dot(both_halves(half), pivot_rel), "leaf", near), "leaf", far)
    y_zero = jnp.concatenate(gather_blocks(y_zero.astype(BF16), "leaf", near), axis=1)
    y_zero, *split_one = tied(y_zero, *halves(back_one))
    x_zero = front_half_at_once(y_zero, (keep, send))
    known_zero = known_pieces(x_zero, groups[0])

    coupling = exchange_sum(picked_product(known_zero, place_up, upper_one), "leaf", groups[1])
    coupling, coupling_root = tied(coupling, picked_product(known_zero, place_root, upper_two))
    z_one = y_one - coupling
    z_one, x_zero = tied(z_one.astype(BF16), x_zero)
    x_one, solution_zero, keep, send = tied(front_half(z_one, split_one), outputs(x_zero), *halves(back_two))
    known_one = known_pieces(x_one, groups[1])

    coupling = coupling_root + picked_product(known_one, place_one, upper_two)
    coupling, other = tied(coupling, partner(x_one, "front", 1))
    coupling, solution_one = tied(exchange_sum(coupling, "leaf", groups[2]), join(x_one, other, core))
    x_two = front_half((y_two - coupling).astype(BF16), (keep, send))
    return solution_zero, solution_one, outputs(x_two)


def solution(mesh):
    by_leaf = P(None, "leaf")
    rows = P("leaf", "front")
    columns = P("front", "leaf")
    return jax.shard_map(
        per_device,
        mesh=mesh,
        in_specs=(by_leaf,) * 3 + (rows,) * 3 + (columns,) * 2 + (rows,) * 2 + (columns,) * 3 + (P(), P()),
        out_specs=(by_leaf,) * 3,
        check_vma=False,
    )
```
